256 devices in a mesh: interval: 8 (over x, y_lo), slab: 32 (over y_hi, z, core).
Axes of the slice: x: 4, y: 4 (y_hi: 2, y_lo: 2; y = y_hi * 2 + y_lo), z: 8, core: 2. Of those that a mesh axis runs over, the one named last changes fastest.
Arguments:
- states: float32 [16, 64, 256, 512], P('interval', 'slab'), may hold values from -0.9 to 0.9
- occupations: int32 [16], P('interval'), may hold values from 1 to 64
- core_density: float32 [64, 256, 512], P('slab'), may hold values from 0.1 to 1
Outputs:
- potential: float32 [64, 256, 512], P('slab', 'interval')
The draws below stay inside these ranges and needn't reach their ends.
All inputs are finite; a program needn't handle non-finite values.
Results may differ from the reference program's by a relative error of at most 0.00002.
Values sent between devices are 32-bit elements; how exact they have to be, the bound alone decides.
No kernel may reach another device: no remote copies, remote signals or barrier semaphores. Data moves between devices by JAX's collectives and lax.ppermute only.
A program may use at most 64 MiB of HBM per device.

```python
import math
import jax
import jax.numpy as jnp
from jax import lax

NX = 256
NY = 512
NZ = 64
NSTATES = 16


def set_ends(array, stream_key, smallest, top_value):
    index_at = [jax.random.randint(jax.random.fold_in(stream_key, axis), (), 0, length) for axis, length in enumerate(array.shape)]
    longest = array.shape.index(max(array.shape))
    neighbour = index_at[:longest] + [(index_at[longest] + 1) % array.shape[longest]] + index_at[longest + 1:]
    return array.at[tuple(index_at)].set(smallest).at[tuple(neighbour)].set(top_value)


def levels(stream_key, shape, split, smallest, high):
    def one(dim, parts):
        draws = jax.random.uniform(jax.random.fold_in(jax.random.fold_in(stream_key, 6), dim), (parts,), jnp.float32, smallest / len(split), high / len(split))
        return jnp.repeat(jnp.exp(draws), shape[dim] // parts).reshape((-1,) + (1,) * (len(shape) - dim - 1))

    loudness = one(*split[0])
    for cut in split[1:]:
        loudness = loudness * one(*cut)
    return loudness


def normal_values(stream_key, dims, deviation, reach, cuts=(), kind=jnp.bfloat16):
    values = deviation * jax.random.normal(stream_key, dims, jnp.float32)
    if cuts:
        values = values * levels(stream_key, dims, cuts, -0.22, 0.18)
    return jnp.clip(values, -reach, reach).astype(kind)


def setup_inputs(seed: int = 0) -> dict:
    seeds = jax.random.split(jax.random.key(seed), 4)
    states = normal_values(seeds[0], (NSTATES, NZ, NX, NY), 0.15, 0.9, ((0, 8), (1, 32)), jnp.float32)
    occupations = set_ends(jax.random.randint(seeds[1], (NSTATES,), 1, 65), jax.random.fold_in(seeds[1], 1), 1, 64).astype(jnp.int32)
    core_density = jnp.clip(jnp.exp(math.log(1.0) - 2.3025851 * jax.random.uniform(seeds[2], (NZ, NX, NY), jnp.float32) ** levels(seeds[2], (NZ, NX, NY), ((0, 32),), -0.2, 0.2)), 0.1, 1.0)
    return {"states": states, "occupations": occupations, "core_density": core_density}


spacing = 0.25
denominator = 64.0
pbe_kappa = 0.804
pbe_mu = 0.2195149727645171
pbe_beta = 0.06672455060314922
pw_alpha = 0.0310907

def deriv_roll(field, axis):
    near = jnp.roll(field, -1, axis) - jnp.roll(field, 1, axis)
    far = jnp.roll(field, -2, axis) - jnp.roll(field, 2, axis)
    return (8.0 * near - far) / (12.0 * spacing)

def pbe_energy(density, grad_sq):
    pbe_gamma = (1.0 - jnp.log(2.0)) / jnp.pi ** 2
    k_fermi = jnp.cbrt(3.0 * jnp.pi ** 2 * density)
    ex_unif = -0.75 * jnp.cbrt(3.0 / jnp.pi) * jnp.cbrt(density)
    s_sq = grad_sq / (4.0 * k_fermi ** 2 * density ** 2)
    f_exch = 1.0 + pbe_kappa - pbe_kappa / (1.0 + pbe_mu * s_sq / pbe_kappa)
    radius = jnp.cbrt(3.0 / (4.0 * jnp.pi * density))
    root_r = jnp.sqrt(radius)
    lower = 2.0 * pw_alpha * (7.5957 * root_r + 3.5876 * radius + 1.6382 * radius * root_r + 0.49294 * radius ** 2)
    e_corr = -2.0 * pw_alpha * (1.0 + 0.2137 * radius) * jnp.log(1.0 + 1.0 / lower)
    k_screen = jnp.sqrt(4.0 * k_fermi / jnp.pi)
    t_sq = grad_sq / (4.0 * k_screen ** 2 * density ** 2)
    factor = pbe_beta / pbe_gamma / jnp.expm1(-e_corr / pbe_gamma)
    ratio_t = (1.0 + factor * t_sq) / (1.0 + factor * t_sq + factor ** 2 * t_sq ** 2)
    h_term = pbe_gamma * jnp.log(1.0 + pbe_beta / pbe_gamma * t_sq * ratio_t)
    return density * (ex_unif * f_exch + e_corr + h_term)

def local_derivs(density, grad_sq):
    return jax.grad(lambda rho, grd: jnp.sum(pbe_energy(rho, grd)), argnums=(0, 1))(density, grad_sq)

def reference(states, occupations, core_density):
    weights = occupations.astype(jnp.float32) / denominator

    def accumulate(index, total):
        one_state = lax.dynamic_index_in_dim(states, index, 0, keepdims=False)
        return total + weights[index] * one_state * one_state
    valence = lax.fori_loop(0, states.shape[0], accumulate, jnp.zeros(states.shape[1:], jnp.float32))
    density = valence + core_density
    grad_z = deriv_roll(density, 0)
    grad_x = deriv_roll(density, 1)
    grad_y = deriv_roll(density, 2)
    grad_sq = grad_z * grad_z + grad_x * grad_x + grad_y * grad_y
    energy_rho, energy_grad = local_derivs(density, grad_sq)
    diverge = deriv_roll(2.0 * energy_grad * grad_z, 0) + deriv_roll(2.0 * energy_grad * grad_x, 1) + deriv_roll(2.0 * energy_grad * grad_y, 2)
    return energy_rho - diverge
```

```python
import functools
import math

import jax
import jax.numpy as jnp
from jax import lax
from jax.experimental import pallas as pl
from jax.experimental.pallas import tpu as pltpu
from jax.sharding import PartitionSpec as P

spacing = 0.25
denominator = 64.0
kappa = 0.804
mu = 0.2195149727645171
beta = 0.06672455060314922
gamma = (1.0 - math.log(2.0)) / math.pi**2
pw_a = 0.0310907
alpha1 = 0.2137
beta_over_gamma = beta / gamma
exch = 0.75 * (3.0 / math.pi) ** (1.0 / 3.0)
rs_unit = (3.0 / (4.0 * math.pi)) ** (1.0 / 3.0)
s_unit = 1.0 / (4.0 * (3.0 * math.pi**2) ** (2.0 / 3.0))
t_unit = math.pi / (16.0 * (3.0 * math.pi**2) ** (1.0 / 3.0))
q1 = 2.0 * pw_a * 7.5957 * rs_unit**0.5
q2 = 2.0 * pw_a * 3.5876 * rs_unit
q3 = 2.0 * pw_a * 1.6382 * rs_unit**1.5
q4 = 2.0 * pw_a * 0.49294 * rs_unit**2

third = 1.0 / (12.0 * spacing)
HALO = 4
VMEM_LIMIT = 40 * 1024 * 1024


def of_density(n, with_energy):
    w = jnp.exp(jnp.log(n) * (-1.0 / 6.0))
    q = w * (q1 + w * (q2 + w * (q3 + w * q4)))
    radius = rs_unit * (w * w)
    slope = 1.0 + alpha1 * radius
    log_term = jnp.log(1.0 + 1.0 / q)
    e_corr = (-2.0 * pw_a) * slope * log_term
    grown = jnp.exp(e_corr * (-1.0 / gamma))
    less = 1.0 / (grown - 1.0)
    factor = beta_over_gamma * less
    if not with_energy:
        return w, factor
    rq = w * (0.5 * q1 + w * (q2 + w * (1.5 * q3 + w * (2.0 * q4))))
    change = (2.0 * pw_a / 3.0) * (alpha1 * radius * log_term - slope * rq / (q * (q + 1.0)))
    return w, factor, e_corr + change, change * factor * (grown * less) * (1.0 / gamma)


def of_gradient(w, factor, g, energy=None):
    w2 = w * w
    w4 = w2 * w2
    w8 = w4 * w4
    s_sq = (s_unit * g) * (w8 * w8)
    t_sq = (t_unit * g) * (w8 * w4 * w2)
    u = factor * t_sq
    up = 1.0 + u
    d = up + u * u
    wide = d + beta_over_gamma * t_sq * up
    inv = 1.0 / (d * wide)
    h_t = beta * (1.0 + 2.0 * u) * inv
    inv_x = 1.0 / (1.0 + (mu / kappa) * s_sq)
    f_s = mu * inv_x * inv_x
    twice = (2.0 * w8) * (t_unit * h_t - (exch * s_unit) * f_s)
    if energy is None:
        return twice
    n, base, change = energy
    h = gamma * jnp.log(wide * wide * inv)
    h_a = -beta * (t_sq * t_sq) * u * (2.0 + u) * inv
    f_x = (1.0 + kappa) - kappa * inv_x
    e_n = base + h + change * h_a - (7.0 / 3.0) * t_sq * h_t
    e_n = e_n - (4.0 / 3.0 * exch) * (n * w4) * (f_x - 2.0 * s_sq * f_s)
    return twice, e_n


def roll(v, shift, axis):
    return pltpu.roll(v, shift % v.shape[axis], axis)


def d_along(v, axis):
    near = roll(v, -1, axis) - roll(v, 1, axis)
    far = roll(v, -2, axis) - roll(v, 2, axis)
    return (8.0 * third) * near - third * far


def d_z(p2, p1, m1, m2):
    return (8.0 * third) * (p1 - m1) - third * (p2 - m2)


def terms_kernel(occ_ref, states_ref, core_ref, out_ref, held, core_held, sems):
    rows = held.shape[2]
    parts, _, wide, _ = out_ref.shape
    own = rows // parts
    pieces = sems.shape[0] - 3
    per = rows // pieces
    me = lax.axis_index("interval")
    flip = lax.rem(lax.axis_index("slab"), 2)
    copies = []
    for k in range(pieces):
        at = pl.ds(k * per, per)
        copies.append(pltpu.make_async_copy(states_ref.at[:, :, at], held.at[:, :, at], sems.at[k]))
    low = pl.multiple_of(lax.rem(me * own + rows - 8, rows), 8)
    mid = pl.multiple_of(me * own, 8)
    top = pl.multiple_of(lax.rem(me * own + own, rows), 8)
    for k, (start, size, to) in enumerate(((low, 8, 0), (mid, own, 8), (top, 8, own + 8))):
        copies.append(
            pltpu.make_async_copy(
                core_ref.at[:, pl.ds(start, size)], core_held.at[:, pl.ds(to, size)], sems.at[pieces + k]
            )
        )
    for c in copies:
        c.start()
    w0 = occ_ref[0].astype(jnp.float32) * (1.0 / denominator)
    w1 = occ_ref[1].astype(jnp.float32) * (1.0 / denominator)
    for k in range(pieces):
        copies[k].wait()
        for i in range(k * per // own, (k + 1) * per // own):
            for p in range(2):
                to = p ^ flip
                for r in range(0, own, 8):
                    a = held[0, p, pl.ds(i * own + r, 8)]
                    b = held[1, p, pl.ds(i * own + r, 8)]
                    t = w0 * a * a + w1 * b * b
                    out_ref[i, to, pl.ds(r + HALO, 8)] = t
                    if r == 0:
                        out_ref[(i - 1) % parts, to, pl.ds(own + HALO, HALO)] = t[:HALO]
                    if r == own - 8:
                        out_ref[(i + 1) % parts, to, pl.ds(0, HALO)] = t[8 - HALO:]
    for c in copies[pieces:]:
        c.wait()
    for p in range(2):
        to = p ^ flip
        out_ref[me, to] = out_ref[me, to] + core_held[p, pl.ds(8 - HALO, wide)]


def density_kernel(s_ref, w_ref, a_ref, base_ref, change_ref, gx_ref, gy_ref):
    rows, cols = s_ref.shape[1:]
    for p in range(2):
        for c in range(0, cols, 128):
            at = pl.ds(c, 128)
            gx_ref[p, :, at] = d_along(s_ref[p, :, at], 0)
        for r in range(0, rows, 8):
            at = pl.ds(r, 8)
            n = s_ref[p, at]
            gy_ref[p, at] = d_along(n, 1)
            w_ref[p, at], a_ref[p, at], base_ref[p, at], change_ref[p, at] = of_density(n, True)


def own_kernel(s_ref, n_ref, w_ref, a_ref, gx_ref, gy_ref, fz_ref, g_ref, twice_ref):
    rows = s_ref.shape[1]
    for r in range(0, rows, 8):
        at = pl.ds(r, 8)
        s = [s_ref[k, at] for k in range(4)]
        n = [n_ref[k, at] for k in range(2)]
        for p, gz in ((0, d_z(s[2], s[1], n[0], n[1])), (1, d_z(s[3], s[2], s[0], n[0]))):
            gx, gy = gx_ref[p, at], gy_ref[p, at]
            g = gz * gz + gx * gx + gy * gy
            twice = of_gradient(w_ref[p, at], a_ref[p, at], g)
            fz_ref[p, at] = twice * gz
            g_ref[p, at] = g
            twice_ref[p, at] = twice


def near_kernel(s_ref, n_ref, w_ref, a_ref, base_ref, change_ref, gx_ref, gy_ref, fz_ref, g_ref, twice_ref, out_ref, gxn, fzn, part):
    rows, cols = s_ref.shape[1:]
    own = rows - 2 * HALO
    for p in range(2):
        for c in range(0, cols, 128):
            at = pl.ds(c, 128)
            gxn[p, :, at] = d_along(n_ref[p, :, at], 0)
            part[p, :, at] = d_along(gx_ref[p, :, at] * twice_ref[p, :, at], 0)
    for r in range(0, rows, 8):
        at = pl.ds(r, 8)
        s = [s_ref[k, at] for k in range(2)]
        n = [n_ref[k, at] for k in range(4)]
        f = []
        for p, gz in ((0, d_z(s[1], s[0], n[1], n[2])), (1, d_z(s[0], n[0], n[2], n[3]))):
            gx, gy = gxn[p, at], d_along(n[p], 1)
            g = gz * gz + gx * gx + gy * gy
            w, factor = of_density(n[p], False)
            f.append(of_gradient(w, factor, g) * gz)
        f0, f1 = fz_ref[0, at], fz_ref[1, at]
        dz = (third * (8.0 * (f1 - f[0]) + f[1]), third * (f[0] - 8.0 * f0))
        for p in range(2):
            twice, e_n = of_gradient(
                w_ref[p, at], a_ref[p, at], g_ref[p, at], (s[p], base_ref[p, at], change_ref[p, at])
            )
            dy = d_along(twice_ref[p, at] * gy_ref[p, at], 1)
            part[p, at] = e_n - (dz[p] + part[p, at] + dy)
    for p in range(2):
        out_ref[p] = part[p, pl.ds(HALO, own)]


def last_kernel(part_ref, fz_ref, out_ref):
    own = part_ref.shape[1]
    flip = lax.rem(lax.axis_index("slab"), 2)
    f0, f1 = fz_ref[0, pl.ds(HALO, own)], fz_ref[1, pl.ds(HALO, own)]
    out_ref[flip] = part_ref[0] - third * f1
    out_ref[1 - flip] = part_ref[1] - third * (f0 - 8.0 * f1)


def call(kernel, outs, *args, scratch=(), specs=None, out_hbm=False):
    f32 = jnp.float32
    if specs is None:
        specs = [pl.BlockSpec(memory_space=pltpu.VMEM)] * len(args)
        args = [pltpu.with_memory_space_constraint(a, pltpu.VMEM) for a in args]
    out_shape = [jax.ShapeDtypeStruct(o, f32) if out_hbm else pltpu.VMEM(o, f32) for o in outs]
    got = pl.pallas_call(
        kernel,
        out_shape=out_shape,
        in_specs=specs,
        out_specs=[pl.BlockSpec(memory_space=pltpu.VMEM)] * len(outs),
        scratch_shapes=list(scratch),
        compiler_params=pltpu.CompilerParams(vmem_limit_bytes=VMEM_LIMIT),
        name=kernel.__name__,
    )(*args)
    return got


def shards(states, occupations, core_density):
    f32 = jnp.float32
    parts = lax.axis_size("interval")
    slabs = lax.axis_size("slab")
    planes, rows, cols = core_density.shape
    own = rows // parts
    wide = own + 2 * HALO
    block = (planes, wide, cols)
    (terms,) = call(
        terms_kernel,
        [(parts, *block)],
        occupations,
        states,
        core_density,
        specs=[pl.BlockSpec(memory_space=pltpu.SMEM), pl.BlockSpec(memory_space=pl.ANY), pl.BlockSpec(memory_space=pl.ANY)],
        scratch=[
            pltpu.VMEM(states.shape, f32),
            pltpu.VMEM((planes, own + 16, cols), f32),
            pltpu.SemaphoreType.DMA((4 + 3,)),
        ],
    )
    density = jnp.sum(lax.all_to_all(terms, "interval", 0, 0), axis=0)
    mates = [(i, i ^ 1) for i in range(slabs)]
    outer = [(i, (i + (1 if i % 2 else -1)) % slabs) for i in range(slabs)]
    mate = lax.ppermute(density, "slab", mates)
    pair = jnp.concatenate([density, mate[::-1]], axis=0)
    beside = lax.ppermute(pair, "slab", outer)
    w, factor, base, change, gx, gy = call(density_kernel, [block] * 6, pair)
    fz, g, twice = call(own_kernel, [block] * 3, pair, beside, w, factor, gx, gy)
    fz_mate = lax.ppermute(fz, "slab", mates)
    (part,) = call(
        near_kernel, [(planes, own, cols)], pair, beside, w, factor, base, change, gx, gy, fz, g, twice,
        scratch=[pltpu.VMEM(block, f32)] * 3,
    )
    (out,) = call(last_kernel, [(planes, own, cols)], part, fz_mate, out_hbm=True)
    return out


def solution(mesh):
    return jax.shard_map(
        shards,
        mesh=mesh,
        in_specs=(P("interval", "slab", None, None), P("interval"), P("slab", None, None)),
        out_specs=P("slab", "interval", None),
        check_vma=False,
    )
```

```python
import functools
import math

import jax
import jax.numpy as jnp
from jax import lax
from jax.experimental import pallas as pl
from jax.experimental.pallas import tpu as pltpu
from jax.sharding import PartitionSpec as P

spacing = 0.25
denominator = 64.0
kappa = 0.804
mu = 0.2195149727645171
beta = 0.06672455060314922
gamma = (1.0 - math.log(2.0)) / math.pi**2
pw_a = 0.0310907
alpha1 = 0.2137
beta_over_gamma = beta / gamma
exch = 0.75 * (3.0 / math.pi) ** (1.0 / 3.0)
rs_unit = (3.0 / (4.0 * math.pi)) ** (1.0 / 3.0)
s_unit = 1.0 / (4.0 * (3.0 * math.pi**2) ** (2.0 / 3.0))
t_unit = math.pi / (16.0 * (3.0 * math.pi**2) ** (1.0 / 3.0))
q1 = 2.0 * pw_a * 7.5957 * rs_unit**0.5
q2 = 2.0 * pw_a * 3.5876 * rs_unit
q3 = 2.0 * pw_a * 1.6382 * rs_unit**1.5
q4 = 2.0 * pw_a * 0.49294 * rs_unit**2

third = 1.0 / (12.0 * spacing)
HALO = 4
VMEM_LIMIT = 40 * 1024 * 1024


def of_density(n, with_energy):
    w = jnp.exp(jnp.log(n) * (-1.0 / 6.0))
    q = w * (q1 + w * (q2 + w * (q3 + w * q4)))
    radius = rs_unit * (w * w)
    slope = 1.0 + alpha1 * radius
    log_term = jnp.log(1.0 + 1.0 / q)
    e_corr = (-2.0 * pw_a) * slope * log_term
    grown = jnp.exp(e_corr * (-1.0 / gamma))
    less = 1.0 / (grown - 1.0)
    factor = beta_over_gamma * less
    if not with_energy:
        return w, factor
    rq = w * (0.5 * q1 + w * (q2 + w * (1.5 * q3 + w * (2.0 * q4))))
    change = (2.0 * pw_a / 3.0) * (alpha1 * radius * log_term - slope * rq / (q * (q + 1.0)))
    return w, factor, e_corr + change, change * factor * (grown * less) * (1.0 / gamma)


def of_gradient(w, factor, g, energy=None):
    w2 = w * w
    w4 = w2 * w2
    w8 = w4 * w4
    s_sq = (s_unit * g) * (w8 * w8)
    t_sq = (t_unit * g) * (w8 * w4 * w2)
    u = factor * t_sq
    up = 1.0 + u
    d = up + u * u
    wide = d + beta_over_gamma * t_sq * up
    inv = 1.0 / (d * wide)
    h_t = beta * (1.0 + 2.0 * u) * inv
    inv_x = 1.0 / (1.0 + (mu / kappa) * s_sq)
    f_s = mu * inv_x * inv_x
    twice = (2.0 * w8) * (t_unit * h_t - (exch * s_unit) * f_s)
    if energy is None:
        return twice
    n, base, change = energy
    h = gamma * jnp.log(wide * wide * inv)
    h_a = -beta * (t_sq * t_sq) * u * (2.0 + u) * inv
    f_x = (1.0 + kappa) - kappa * inv_x
    e_n = base + h + change * h_a - (7.0 / 3.0) * t_sq * h_t
    e_n = e_n - (4.0 / 3.0 * exch) * (n * w4) * (f_x - 2.0 * s_sq * f_s)
    return twice, e_n


def roll(v, shift, axis):
    return pltpu.roll(v, shift % v.shape[axis], axis)


def d_along(v, axis):
    near = roll(v, -1, axis) - roll(v, 1, axis)
    far = roll(v, -2, axis) - roll(v, 2, axis)
    return (8.0 * third) * near - third * far


def d_z(p2, p1, m1, m2):
    return (8.0 * third) * (p1 - m1) - third * (p2 - m2)


def terms_kernel(occ_ref, states_ref, core_ref, out_ref, occ_held, held, core_held, sems):
    rows = held.shape[2]
    parts, _, wide, _ = out_ref.shape
    own = rows // parts
    pieces = sems.shape[0] - 4
    per = rows // pieces
    me = lax.axis_index("interval")
    flip = lax.rem(lax.axis_index("slab"), 2)
    first = pltpu.make_async_copy(occ_ref, occ_held, sems.at[pieces + 3])
    first.start()
    copies = []
    for k in range(pieces):
        at = pl.ds(k * per, per)
        copies.append(pltpu.make_async_copy(states_ref.at[:, :, at], held.at[:, :, at], sems.at[k]))
    low = pl.multiple_of(lax.rem(me * own + rows - 8, rows), 8)
    mid = pl.multiple_of(me * own, 8)
    top = pl.multiple_of(lax.rem(me * own + own, rows), 8)
    for k, (start, size, to) in enumerate(((low, 8, 0), (mid, own, 8), (top, 8, own + 8))):
        copies.append(
            pltpu.make_async_copy(
                core_ref.at[:, pl.ds(start, size)], core_held.at[:, pl.ds(to, size)], sems.at[pieces + k]
            )
        )
    for c in copies:
        c.start()
    first.wait()
    w0 = occ_held[0].astype(jnp.float32) * (1.0 / denominator)
    w1 = occ_held[1].astype(jnp.float32) * (1.0 / denominator)
    for k in range(pieces):
        copies[k].wait()
        for i in range(k * per // own, (k + 1) * per // own):
            for p in range(2):
                to = p ^ flip
                for r in range(0, own, 8):
                    a = held[0, p, pl.ds(i * own + r, 8)]
                    b = held[1, p, pl.ds(i * own + r, 8)]
                    t = w0 * a * a + w1 * b * b
                    out_ref[i, to, pl.ds(r + HALO, 8)] = t
                    if r == 0:
                        out_ref[(i - 1) % parts, to, pl.ds(own + HALO, HALO)] = t[:HALO]
                    if r == own - 8:
                        out_ref[(i + 1) % parts, to, pl.ds(0, HALO)] = t[8 - HALO:]
    for c in copies[pieces:]:
        c.wait()
    for p in range(2):
        to = p ^ flip
        out_ref[me, to] = out_ref[me, to] + core_held[p, pl.ds(8 - HALO, wide)]


def x_slopes(field, slopes):
    for p in range(2):
        for c in range(0, field.shape[2], 128):
            at = pl.ds(c, 128)
            slopes[p, :, at] = d_along(field[p, :, at], 0)


def own_kernel(s_ref, w_ref, a_ref, base_ref, change_ref, gx_ref, gy_ref):
    x_slopes(s_ref, gx_ref)
    for p in range(2):
        for r in range(0, s_ref.shape[1], 8):
            at = pl.ds(r, 8)
            n = s_ref[p, at]
            gy_ref[p, at] = d_along(n, 1)
            w_ref[p, at], a_ref[p, at], base_ref[p, at], change_ref[p, at] = of_density(n, True)


def mate_kernel(m_ref, w_ref, a_ref, flat_ref):
    x_slopes(m_ref, flat_ref)
    for p in range(2):
        for r in range(0, m_ref.shape[1], 8):
            at = pl.ds(r, 8)
            n = m_ref[p, at]
            gx, gy = flat_ref[p, at], d_along(n, 1)
            flat_ref[p, at] = gx * gx + gy * gy
            w_ref[p, at], a_ref[p, at] = of_density(n, False)


def ahead_kernel(s_ref, m_ref, far_ref, w_ref, a_ref, flat_ref, fz_ref):
    for r in range(0, s_ref.shape[1], 8):
        at = pl.ds(r, 8)
        s = (s_ref[0, at], s_ref[1, at], m_ref[1, at], m_ref[0, at], far_ref[0, at], far_ref[1, at])
        for p, gz in ((1, d_z(s[4], s[3], s[1], s[0])), (0, d_z(s[5], s[4], s[2], s[1]))):
            g = gz * gz + flat_ref[p, at]
            fz_ref[1 - p, at] = of_gradient(w_ref[p, at], a_ref[p, at], g) * gz


def last_kernel(
    s_ref, m_ref, n_ref, b_ref, w_ref, a_ref, base_ref, change_ref, gx_ref, gy_ref, fz_ref, out_ref, gxn, fx, part
):
    rows, cols = s_ref.shape[1:]
    own = rows - 2 * HALO
    flip = lax.rem(lax.axis_index("slab"), 2)
    x_slopes(n_ref, gxn)
    for r in range(0, rows, 8):
        at = pl.ds(r, 8)
        s = (s_ref[0, at], s_ref[1, at], m_ref[1, at], m_ref[0, at])
        n = (n_ref[0, at], n_ref[1, at], b_ref[1, at], b_ref[0, at])
        f = []
        for p, gz in ((0, d_z(s[1], s[0], n[1], n[2])), (1, d_z(s[0], n[0], n[2], n[3]))):
            gx, gy = gxn[p, at], d_along(n[p], 1)
            w, factor = of_density(n[p], False)
            f.append(of_gradient(w, factor, gz * gz + gx * gx + gy * gy) * gz)
        o = []
        for p, gz in ((0, d_z(s[2], s[1], n[0], n[1])), (1, d_z(s[3], s[2], s[0], n[0]))):
            gx, gy = gx_ref[p, at], gy_ref[p, at]
            g = gz * gz + gx * gx + gy * gy
            twice, e_n = of_gradient(
                w_ref[p, at], a_ref[p, at], g, (s[p], base_ref[p, at], change_ref[p, at])
            )
            fx[p, at] = twice * gx
            o.append(twice * gz)
            part[p, at] = e_n - d_along(twice * gy, 1)
        f2, f3 = fz_ref[0, at], fz_ref[1, at]
        part[0, at] = part[0, at] - d_z(f2, o[1], f[0], f[1])
        part[1, at] = part[1, at] - d_z(f3, f2, o[0], f[0])
    x_slopes(fx, gxn)
    for p in range(2):
        out_ref[p ^ flip] = part[p, pl.ds(HALO, own)] - gxn[p, pl.ds(HALO, own)]


def call(kernel, outs, *args, scratch=(), out_hbm=False, flops=0):
    f32 = jnp.float32
    return pl.pallas_call(
        kernel,
        out_shape=[jax.ShapeDtypeStruct(o, f32) if out_hbm else pltpu.VMEM(o, f32) for o in outs],
        in_specs=[pl.BlockSpec(memory_space=pltpu.VMEM)] * len(args),
        out_specs=[pl.BlockSpec(memory_space=pltpu.VMEM)] * len(outs),
        scratch_shapes=list(scratch),
        compiler_params=pltpu.CompilerParams(vmem_limit_bytes=VMEM_LIMIT),
        cost_estimate=pl.CostEstimate(
            flops=flops, bytes_accessed=4 * sum(math.prod(o) for o in outs), transcendentals=flops // 32
        ),
        name=kernel.__name__,
    )(*[pltpu.with_memory_space_constraint(a, pltpu.VMEM) for a in args])


def shards(states, occupations, core_density):
    f32 = jnp.float32
    parts = lax.axis_size("interval")
    slabs = lax.axis_size("slab")
    planes, rows, cols = core_density.shape
    own = rows // parts
    wide = own + 2 * HALO
    block = (planes, wide, cols)
    pieces = 4
    (terms,) = pl.pallas_call(
        terms_kernel,
        out_shape=[pltpu.VMEM((parts, *block), f32)],
        in_specs=[pl.BlockSpec(memory_space=pltpu.HBM)] * 3,
        out_specs=[pl.BlockSpec(memory_space=pltpu.VMEM)],
        scratch_shapes=[
            pltpu.SMEM(occupations.shape, jnp.int32),
            pltpu.VMEM(states.shape, f32),
            pltpu.VMEM((planes, own + 16, cols), f32),
            pltpu.SemaphoreType.DMA((pieces + 4,)),
        ],
        compiler_params=pltpu.CompilerParams(vmem_limit_bytes=VMEM_LIMIT),
        name="terms_kernel",
    )(*[pltpu.with_memory_space_constraint(a, pltpu.HBM) for a in (occupations, states, core_density)])
    density = jnp.sum(lax.all_to_all(terms, "interval", 0, 0), axis=0)
    chips = slabs // 2
    beside = lambda q, odd: (q + (1 if q % 2 == odd else -1)) % chips
    odd_pairs = [(s, 2 * beside(s // 2, 1) + s % 2) for s in range(slabs)]
    even_pairs = [(s, 2 * beside(s // 2, 0) + s % 2) for s in range(slabs)]
    mates = [(s, s ^ 1) for s in range(slabs)]
    from_even = lax.ppermute(density, "slab", even_pairs)
    from_odd = lax.ppermute(density, "slab", odd_pairs)
    mate = lax.ppermute(density, "slab", mates)
    w, factor, base, change, gx, gy = call(own_kernel, [block] * 6, density, flops=100_000_000)
    w_m, factor_m, flat_m = call(mate_kernel, [block] * 3, mate, flops=100_000_000)
    from_odd, from_even, w, w_m = lax.optimization_barrier((from_odd, from_even, w, w_m))
    at = lax.axis_index("slab")
    odd_ahead = lax.rem(at // 2 + at, 2) == 1
    ahead = jnp.where(odd_ahead, from_odd, from_even)
    behind = jnp.where(odd_ahead, from_even, from_odd)
    near = lax.ppermute(ahead, "slab", mates)
    (fz,) = call(ahead_kernel, [block], density, mate, ahead, w_m, factor_m, flat_m, flops=50_000_000)
    (out,) = call(
        last_kernel, [(planes, own, cols)],
        density, mate, near, behind, w, factor, base, change, gx, gy, fz,
        scratch=[pltpu.VMEM(block, f32)] * 3, out_hbm=True,
    )
    return out


def solution(mesh):
    return jax.shard_map(
        shards,
        mesh=mesh,
        in_specs=(P("interval", "slab", None, None), P("interval"), P("slab", None, None)),
        out_specs=P("slab", "interval", None),
        check_vma=False,
    )
```

```python
import functools
import math

import jax
import jax.numpy as jnp
from jax import lax
from jax.experimental import pallas as pl
from jax.experimental.pallas import tpu as pltpu
from jax.sharding import PartitionSpec as P

spacing = 0.25
denominator = 64.0
kappa = 0.804
mu = 0.2195149727645171
beta = 0.06672455060314922
gamma = (1.0 - math.log(2.0)) / math.pi**2
pw_a = 0.0310907
alpha1 = 0.2137
beta_over_gamma = beta / gamma
exch = 0.75 * (3.0 / math.pi) ** (1.0 / 3.0)
rs_unit = (3.0 / (4.0 * math.pi)) ** (1.0 / 3.0)
s_unit = 1.0 / (4.0 * (3.0 * math.pi**2) ** (2.0 / 3.0))
t_unit = math.pi / (16.0 * (3.0 * math.pi**2) ** (1.0 / 3.0))
q1 = 2.0 * pw_a * 7.5957 * rs_unit**0.5
q2 = 2.0 * pw_a * 3.5876 * rs_unit
q3 = 2.0 * pw_a * 1.6382 * rs_unit**1.5
q4 = 2.0 * pw_a * 0.49294 * rs_unit**2

third = 1.0 / (12.0 * spacing)
HALO = 4
VMEM_LIMIT = 40 * 1024 * 1024


def of_density(n, with_energy):
    w = jnp.exp(jnp.log(n) * (-1.0 / 6.0))
    q = w * (q1 + w * (q2 + w * (q3 + w * q4)))
    radius = rs_unit * (w * w)
    slope = 1.0 + alpha1 * radius
    log_term = jnp.log(1.0 + 1.0 / q)
    e_corr = (-2.0 * pw_a) * slope * log_term
    grown = jnp.exp(e_corr * (-1.0 / gamma))
    less = 1.0 / (grown - 1.0)
    factor = beta_over_gamma * less
    if not with_energy:
        return w, factor
    rq = w * (0.5 * q1 + w * (q2 + w * (1.5 * q3 + w * (2.0 * q4))))
    change = (2.0 * pw_a / 3.0) * (alpha1 * radius * log_term - slope * rq / (q * (q + 1.0)))
    return w, factor, e_corr + change, change * factor * (grown * less) * (1.0 / gamma)


def of_gradient(w, factor, g, energy=None):
    w2 = w * w
    w4 = w2 * w2
    w8 = w4 * w4
    s_sq = (s_unit * g) * (w8 * w8)
    t_sq = (t_unit * g) * (w8 * w4 * w2)
    u = factor * t_sq
    up = 1.0 + u
    d = up + u * u
    wide = d + beta_over_gamma * t_sq * up
    inv = 1.0 / (d * wide)
    h_t = beta * (1.0 + 2.0 * u) * inv
    inv_x = 1.0 / (1.0 + (mu / kappa) * s_sq)
    f_s = mu * inv_x * inv_x
    twice = (2.0 * w8) * (t_unit * h_t - (exch * s_unit) * f_s)
    if energy is None:
        return twice
    n, base, change = energy
    h = gamma * jnp.log(wide * wide * inv)
    h_a = -beta * (t_sq * t_sq) * u * (2.0 + u) * inv
    f_x = (1.0 + kappa) - kappa * inv_x
    e_n = base + h + change * h_a - (7.0 / 3.0) * t_sq * h_t
    e_n = e_n - (4.0 / 3.0 * exch) * (n * w4) * (f_x - 2.0 * s_sq * f_s)
    return twice, e_n


def roll(v, shift, axis):
    return pltpu.roll(v, shift % v.shape[axis], axis)


def d_along(v, axis):
    near = roll(v, -1, axis) - roll(v, 1, axis)
    far = roll(v, -2, axis) - roll(v, 2, axis)
    return (8.0 * third) * near - third * far


def d_z(p2, p1, m1, m2):
    return (8.0 * third) * (p1 - m1) - third * (p2 - m2)


def terms_kernel(occ_ref, states_ref, core_ref, out_ref, occ_held, held, core_held, sems):
    rows = held.shape[2]
    parts = out_ref.shape[0]
    own = rows // parts
    pieces = sems.shape[0] - 4
    per = rows // pieces
    me = lax.axis_index("interval")
    flip = lax.rem(lax.axis_index("slab"), 2)
    first = pltpu.make_async_copy(occ_ref, occ_held, sems.at[pieces + 3])
    first.start()
    copies = []
    for k in range(pieces):
        at = pl.ds(k * per, per)
        copies.append(pltpu.make_async_copy(states_ref.at[:, :, at], held.at[:, :, at], sems.at[k]))
    low = pl.multiple_of(lax.rem(me * own + rows - 8, rows), 8)
    mid = pl.multiple_of(me * own, 8)
    top = pl.multiple_of(lax.rem(me * own + own, rows), 8)
    for k, (start, size, to) in enumerate(((mid, own, 0), (top, 8, own), (low, 8, own + 8))):
        copies.append(
            pltpu.make_async_copy(
                core_ref.at[:, pl.ds(start, size)], core_held.at[:, pl.ds(to, size)], sems.at[pieces + k]
            )
        )
    for c in copies:
        c.start()
    first.wait()
    w0 = occ_held[0].astype(jnp.float32) * (1.0 / denominator)
    w1 = occ_held[1].astype(jnp.float32) * (1.0 / denominator)
    for k in range(pieces):
        copies[k].wait()
        for i in range(k * per // own, (k + 1) * per // own):
            for p in range(2):
                to = p ^ flip
                for r in range(0, own, 8):
                    a = held[0, p, pl.ds(i * own + r, 8)]
                    b = held[1, p, pl.ds(i * own + r, 8)]
                    t = w0 * a * a + w1 * b * b
                    out_ref[i, to, pl.ds(r, 8)] = t
                    if r == 0:
                        out_ref[(i - 1) % parts, to, pl.ds(own, HALO)] = t[:HALO]
                    if r == own - 8:
                        out_ref[(i + 1) % parts, to, pl.ds(own + HALO, HALO)] = t[HALO:]
    for c in copies[pieces:]:
        c.wait()
    for p in range(2):
        to = p ^ flip
        for to_row, size, row in ((0, own, 0), (own, HALO, own), (own + HALO, HALO, own + 8 + HALO)):
            at = pl.ds(to_row, size)
            out_ref[me, to, at] = out_ref[me, to, at] + core_held[p, pl.ds(row, size)]


def x_slopes(field, slopes):
    for p in range(2):
        for c in range(0, field.shape[2], 128):
            at = pl.ds(c, 128)
            slopes[p, :, at] = d_along(field[p, :, at], 0)


def own_kernel(s_ref, w_ref, a_ref, base_ref, change_ref, gx_ref, gy_ref):
    x_slopes(s_ref, gx_ref)
    for p in range(2):
        for r in range(0, s_ref.shape[1], 8):
            at = pl.ds(r, 8)
            n = s_ref[p, at]
            gy_ref[p, at] = d_along(n, 1)
            if r < s_ref.shape[1] - 2 * HALO:
                w_ref[p, at], a_ref[p, at], base_ref[p, at], change_ref[p, at] = of_density(n, True)
            else:
                w_ref[p, at], a_ref[p, at] = of_density(n, False)


def flux_kernel(s_ref, m_ref, n_ref, w_ref, a_ref, gx_ref, gy_ref, fz_ref, g_ref, twice_ref):
    rows = s_ref.shape[1]
    own = rows - 2 * HALO
    for r in range(0, rows, 8):
        at = pl.ds(r, 8)
        s = (s_ref[0, at], s_ref[1, at], m_ref[1, at], m_ref[0, at])
        n = (n_ref[0, at], n_ref[1, at])
        for p, gz in ((0, d_z(s[2], s[1], n[0], n[1])), (1, d_z(s[3], s[2], s[0], n[0]))):
            gx, gy = gx_ref[p, at], gy_ref[p, at]
            g = gz * gz + gx * gx + gy * gy
            twice = of_gradient(w_ref[p, at], a_ref[p, at], g)
            g_ref[p, at] = g
            twice_ref[p, at] = twice
            if r < own:
                fz_ref[p, at] = twice * gz


def flat_kernel(
    s_ref, n_ref, w_ref, a_ref, base_ref, change_ref, gx_ref, gy_ref, g_ref, twice_ref,
    part_ref, wn_ref, an_ref, flat_ref, slopes, fx
):
    rows = s_ref.shape[1]
    own = rows - 2 * HALO
    for p in range(2):
        for r in range(0, rows, 8):
            at = pl.ds(r, 8)
            fx[p, at] = twice_ref[p, at] * gx_ref[p, at]
    x_slopes(fx, slopes)
    x_slopes(n_ref, fx)
    for r in range(0, own, 8):
        at = pl.ds(r, 8)
        for p in range(2):
            _, e_n = of_gradient(
                w_ref[p, at], a_ref[p, at], g_ref[p, at], (s_ref[p, at], base_ref[p, at], change_ref[p, at])
            )
            part_ref[p, at] = e_n - slopes[p, at] - d_along(twice_ref[p, at] * gy_ref[p, at], 1)
            n = n_ref[p, at]
            gx, gy = fx[p, at], d_along(n, 1)
            flat_ref[p, at] = gx * gx + gy * gy
            wn_ref[p, at], an_ref[p, at] = of_density(n, False)


def last_kernel(s_ref, n_ref, b_ref, part_ref, wn_ref, an_ref, flat_ref, fz_ref, fm_ref, out_ref):
    own = part_ref.shape[1]
    flip = lax.rem(lax.axis_index("slab"), 2)
    for r in range(0, own, 8):
        at = pl.ds(r, 8)
        s = (s_ref[0, at], s_ref[1, at])
        n = (n_ref[0, at], n_ref[1, at], b_ref[1, at], b_ref[0, at])
        f = []
        for p, gz in ((0, d_z(s[1], s[0], n[1], n[2])), (1, d_z(s[0], n[0], n[2], n[3]))):
            f.append(of_gradient(wn_ref[p, at], an_ref[p, at], gz * gz + flat_ref[p, at]) * gz)
        f0, f1 = fz_ref[0, at], fz_ref[1, at]
        f2, f3 = -fm_ref[1, at], -fm_ref[0, at]
        out_ref[flip, at] = part_ref[0, at] - d_z(f2, f1, f[0], f[1])
        out_ref[1 - flip, at] = part_ref[1, at] - d_z(f3, f2, f0, f[0])


def call(kernel, outs, *args, scratch=(), out_hbm=False, flops=0):
    f32 = jnp.float32
    return pl.pallas_call(
        kernel,
        out_shape=[jax.ShapeDtypeStruct(o, f32) if out_hbm else pltpu.VMEM(o, f32) for o in outs],
        in_specs=[pl.BlockSpec(memory_space=pltpu.VMEM)] * len(args),
        out_specs=[pl.BlockSpec(memory_space=pltpu.VMEM)] * len(outs),
        scratch_shapes=list(scratch),
        compiler_params=pltpu.CompilerParams(vmem_limit_bytes=VMEM_LIMIT),
        cost_estimate=pl.CostEstimate(
            flops=flops, bytes_accessed=4 * sum(math.prod(o) for o in outs), transcendentals=flops // 32
        ),
        name=kernel.__name__,
    )(*[pltpu.with_memory_space_constraint(a, pltpu.VMEM) for a in args])


def shards(states, occupations, core_density):
    f32 = jnp.float32
    parts = lax.axis_size("interval")
    slabs = lax.axis_size("slab")
    planes, rows, cols = core_density.shape
    own = rows // parts
    wide = own + 2 * HALO
    block = (planes, wide, cols)
    pieces = 4
    (terms,) = pl.pallas_call(
        terms_kernel,
        out_shape=[pltpu.VMEM((parts, *block), f32)],
        in_specs=[pl.BlockSpec(memory_space=pltpu.HBM)] * 3,
        out_specs=[pl.BlockSpec(memory_space=pltpu.VMEM)],
        scratch_shapes=[
            pltpu.SMEM(occupations.shape, jnp.int32),
            pltpu.VMEM(states.shape, f32),
            pltpu.VMEM((planes, own + 16, cols), f32),
            pltpu.SemaphoreType.DMA((pieces + 4,)),
        ],
        compiler_params=pltpu.CompilerParams(vmem_limit_bytes=VMEM_LIMIT),
        name="terms_kernel",
    )(*[pltpu.with_memory_space_constraint(a, pltpu.HBM) for a in (occupations, states, core_density)])
    density = jnp.sum(lax.all_to_all(terms, "interval", 0, 0), axis=0)
    chips = slabs // 2
    beside = lambda q, odd: (q + (1 if q % 2 == odd else -1)) % chips
    odd_pairs = [(s, 2 * beside(s // 2, 1) + 1 - s % 2) for s in range(slabs)]
    even_pairs = [(s, 2 * beside(s // 2, 0) + 1 - s % 2) for s in range(slabs)]
    mates = [(s, s ^ 1) for s in range(slabs)]
    from_even = lax.ppermute(density, "slab", even_pairs)
    from_odd = lax.ppermute(density, "slab", odd_pairs)
    mate = lax.ppermute(density, "slab", mates)
    w, factor, base, change, gx, gy = call(own_kernel, [block] * 6, density, flops=100_000_000)
    from_odd, from_even, w = lax.optimization_barrier((from_odd, from_even, w))
    at = lax.axis_index("slab")
    odd_near = lax.rem(at // 2 + at, 2) == 0
    near = jnp.where(odd_near, from_odd, from_even)
    other = jnp.where(odd_near, from_even, from_odd)[:, :own]
    far = lax.ppermute(other, "slab", mates)
    kept = (planes, own, cols)
    fz, g, twice = call(
        flux_kernel, [kept, block, block], density, mate, near, w, factor, gx, gy, flops=50_000_000
    )
    fz_mate = lax.ppermute(fz, "slab", mates)
    part, w_n, factor_n, flat_n = call(
        flat_kernel, [kept] * 4, density, near, w, factor, base, change, gx, gy, g, twice,
        scratch=[pltpu.VMEM(block, f32)] * 2, flops=100_000_000,
    )
    far, fz_mate, part = lax.optimization_barrier((far, fz_mate, part))
    (out,) = call(
        last_kernel, [kept], density, near, far, part, w_n, factor_n, flat_n, fz, fz_mate, out_hbm=True
    )
    return out


def solution(mesh):
    return jax.shard_map(
        shards,
        mesh=mesh,
        in_specs=(P("interval", "slab", None, None), P("interval"), P("slab", None, None)),
        out_specs=P("slab", "interval", None),
        check_vma=False,
    )
```

```python
import functools
import math

import jax
import jax.numpy as jnp
from jax import lax
from jax.experimental import pallas as pl
from jax.experimental.pallas import tpu as pltpu
from jax.sharding import PartitionSpec as P

spacing = 0.25
denominator = 64.0
kappa = 0.804
mu = 0.2195149727645171
beta = 0.06672455060314922
gamma = (1.0 - math.log(2.0)) / math.pi**2
pw_a = 0.0310907
alpha1 = 0.2137
beta_over_gamma = beta / gamma
exch = 0.75 * (3.0 / math.pi) ** (1.0 / 3.0)
rs_unit = (3.0 / (4.0 * math.pi)) ** (1.0 / 3.0)
s_unit = 1.0 / (4.0 * (3.0 * math.pi**2) ** (2.0 / 3.0))
t_unit = math.pi / (16.0 * (3.0 * math.pi**2) ** (1.0 / 3.0))
q1 = 2.0 * pw_a * 7.5957 * rs_unit**0.5
q2 = 2.0 * pw_a * 3.5876 * rs_unit
q3 = 2.0 * pw_a * 1.6382 * rs_unit**1.5
q4 = 2.0 * pw_a * 0.49294 * rs_unit**2

third = 1.0 / (12.0 * spacing)
HALO = 4
VMEM_LIMIT = 40 * 1024 * 1024


def of_density(n, with_energy):
    w = jnp.exp(jnp.log(n) * (-1.0 / 6.0))
    q = w * (q1 + w * (q2 + w * (q3 + w * q4)))
    radius = rs_unit * (w * w)
    slope = 1.0 + alpha1 * radius
    log_term = jnp.log(1.0 + 1.0 / q)
    e_corr = (-2.0 * pw_a) * slope * log_term
    grown = jnp.exp(e_corr * (-1.0 / gamma))
    less = 1.0 / (grown - 1.0)
    factor = beta_over_gamma * less
    if not with_energy:
        return w, factor
    rq = w * (0.5 * q1 + w * (q2 + w * (1.5 * q3 + w * (2.0 * q4))))
    change = (2.0 * pw_a / 3.0) * (alpha1 * radius * log_term - slope * rq / (q * (q + 1.0)))
    return w, factor, e_corr + change, change * factor * (grown * less) * (1.0 / gamma)


def of_gradient(w, factor, g, energy=None):
    w2 = w * w
    w4 = w2 * w2
    w8 = w4 * w4
    s_sq = (s_unit * g) * (w8 * w8)
    t_sq = (t_unit * g) * (w8 * w4 * w2)
    u = factor * t_sq
    up = 1.0 + u
    d = up + u * u
    wide = d + beta_over_gamma * t_sq * up
    inv = 1.0 / (d * wide)
    h_t = beta * (1.0 + 2.0 * u) * inv
    inv_x = 1.0 / (1.0 + (mu / kappa) * s_sq)
    f_s = mu * inv_x * inv_x
    twice = (2.0 * w8) * (t_unit * h_t - (exch * s_unit) * f_s)
    if energy is None:
        return twice
    n, base, change = energy
    h = gamma * jnp.log(wide * wide * inv)
    h_a = -beta * (t_sq * t_sq) * u * (2.0 + u) * inv
    f_x = (1.0 + kappa) - kappa * inv_x
    e_n = base + h + change * h_a - (7.0 / 3.0) * t_sq * h_t
    e_n = e_n - (4.0 / 3.0 * exch) * (n * w4) * (f_x - 2.0 * s_sq * f_s)
    return twice, e_n


def roll(v, shift, axis):
    return pltpu.roll(v, shift % v.shape[axis], axis)


def d_along(v, axis):
    near = roll(v, -1, axis) - roll(v, 1, axis)
    far = roll(v, -2, axis) - roll(v, 2, axis)
    return (8.0 * third) * near - third * far


def d_z(p2, p1, m1, m2):
    return (8.0 * third) * (p1 - m1) - third * (p2 - m2)


def terms_kernel(groups, occ_ref, states_ref, core_ref, *refs):
    *outs, occ_held, held, core_held, sems = refs
    rows = held.shape[2]
    parts = sum(len(group) for group in groups)
    own = rows // parts
    me = lax.axis_index("interval")
    flip = lax.rem(lax.axis_index("slab"), 2)
    first = pltpu.make_async_copy(occ_ref, occ_held, sems.at[0])
    first.start()
    copies = []
    pieces = sems.shape[0] - 4
    per = rows // pieces
    for k in range(pieces):
        at = pl.ds(k * per, per)
        copies.append(pltpu.make_async_copy(states_ref.at[:, :, at], held.at[:, :, at], sems.at[4 + k]))
    low = pl.multiple_of(lax.rem(me * own + rows - 8, rows), 8)
    mid = pl.multiple_of(me * own, 8)
    top = pl.multiple_of(lax.rem(me * own + own, rows), 8)
    for k, (start, size, to) in enumerate(((mid, own, 0), (top, 8, own), (low, 8, own + 8))):
        copies.append(
            pltpu.make_async_copy(
                core_ref.at[:, pl.ds(start, size)], core_held.at[:, pl.ds(to, size)], sems.at[1 + k]
            )
        )
    for c in copies:
        c.start()
    first.wait()
    w0 = occ_held[0].astype(jnp.float32) * (1.0 / denominator)
    w1 = occ_held[1].astype(jnp.float32) * (1.0 / denominator)

    def term(p, row):
        at = pl.ds(pl.multiple_of(row, 8), 8)
        a, b = held[0, p, at], held[1, p, at]
        return w0 * a * a + w1 * b * b

    for c in copies[:pieces]:
        c.wait()
    places = [(k, out, 2 * j) for group, out in zip(groups, outs) for j, k in enumerate(group)]
    for k, out, shift in places:
        i = me ^ k
        up = lax.rem(i + 1, parts) * own
        down = lax.rem(i + parts - 1, parts) * own + own - 8
        if k == 0:
            for c in copies[pieces:]:
                c.wait()
        for p in range(2):
            to = shift + (p ^ flip)
            for r in range(0, own, 8):
                t = term(p, i * own + r)
                if k == 0:
                    t = t + core_held[p, pl.ds(r, 8)]
                out[to, pl.ds(r, 8)] = t
            t, b = term(p, up), term(p, down)
            if k == 0:
                t, b = t + core_held[p, pl.ds(own, 8)], b + core_held[p, pl.ds(own + 8, 8)]
            out[to, pl.ds(own, HALO)] = t[:HALO]
            out[to, pl.ds(own + HALO, HALO)] = b[HALO:]


def x_slopes(field, slopes):
    for p in range(2):
        for c in range(0, field.shape[2], 128):
            at = pl.ds(c, 128)
            slopes[p, :, at] = d_along(field[p, :, at], 0)


def own_kernel(s_ref, w_ref, a_ref, base_ref, change_ref, gx_ref, gy_ref):
    x_slopes(s_ref, gx_ref)
    for p in range(2):
        for r in range(0, s_ref.shape[1], 8):
            at = pl.ds(r, 8)
            n = s_ref[p, at]
            gy_ref[p, at] = d_along(n, 1)
            if r < s_ref.shape[1] - 2 * HALO:
                w_ref[p, at], a_ref[p, at], base_ref[p, at], change_ref[p, at] = of_density(n, True)
            else:
                w_ref[p, at], a_ref[p, at] = of_density(n, False)


def flux_kernel(s_ref, m_ref, n_ref, w_ref, a_ref, gx_ref, gy_ref, fz_ref, g_ref, twice_ref):
    rows = s_ref.shape[1]
    own = rows - 2 * HALO
    for r in range(0, rows, 8):
        at = pl.ds(r, 8)
        s = (s_ref[0, at], s_ref[1, at], m_ref[1, at], m_ref[0, at])
        n = (n_ref[0, at], n_ref[1, at])
        for p, gz in ((0, d_z(s[2], s[1], n[0], n[1])), (1, d_z(s[3], s[2], s[0], n[0]))):
            gx, gy = gx_ref[p, at], gy_ref[p, at]
            g = gz * gz + gx * gx + gy * gy
            twice = of_gradient(w_ref[p, at], a_ref[p, at], g)
            g_ref[p, at] = g
            twice_ref[p, at] = twice
            if r < own:
                fz_ref[p, at] = twice * gz


def flat_kernel(
    s_ref, n_ref, w_ref, a_ref, base_ref, change_ref, gx_ref, gy_ref, g_ref, twice_ref,
    part_ref, wn_ref, an_ref, flat_ref, slopes, fx
):
    rows = s_ref.shape[1]
    own = rows - 2 * HALO
    for p in range(2):
        for r in range(0, rows, 8):
            at = pl.ds(r, 8)
            fx[p, at] = twice_ref[p, at] * gx_ref[p, at]
    x_slopes(fx, slopes)
    x_slopes(n_ref, fx)
    for r in range(0, own, 8):
        at = pl.ds(r, 8)
        for p in range(2):
            _, e_n = of_gradient(
                w_ref[p, at], a_ref[p, at], g_ref[p, at], (s_ref[p, at], base_ref[p, at], change_ref[p, at])
            )
            part_ref[p, at] = e_n - slopes[p, at] - d_along(twice_ref[p, at] * gy_ref[p, at], 1)
            n = n_ref[p, at]
            gx, gy = fx[p, at], d_along(n, 1)
            flat_ref[p, at] = gx * gx + gy * gy
            wn_ref[p, at], an_ref[p, at] = of_density(n, False)


def last_kernel(s_ref, n_ref, b_ref, part_ref, wn_ref, an_ref, flat_ref, fz_ref, fm_ref, out_ref):
    own = part_ref.shape[1]
    flip = lax.rem(lax.axis_index("slab"), 2)
    for r in range(0, own, 8):
        at = pl.ds(r, 8)
        s = (s_ref[0, at], s_ref[1, at])
        n = (n_ref[0, at], n_ref[1, at], b_ref[1, at], b_ref[0, at])
        f = []
        for p, gz in ((0, d_z(s[1], s[0], n[1], n[2])), (1, d_z(s[0], n[0], n[2], n[3]))):
            f.append(of_gradient(wn_ref[p, at], an_ref[p, at], gz * gz + flat_ref[p, at]) * gz)
        f0, f1 = fz_ref[0, at], fz_ref[1, at]
        f2, f3 = -fm_ref[1, at], -fm_ref[0, at]
        out_ref[flip, at] = part_ref[0, at] - d_z(f2, f1, f[0], f[1])
        out_ref[1 - flip, at] = part_ref[1, at] - d_z(f3, f2, f0, f[0])


def call(kernel, outs, *args, scratch=(), out_hbm=False, flops=0):
    f32 = jnp.float32
    return pl.pallas_call(
        kernel,
        out_shape=[jax.ShapeDtypeStruct(o, f32) if out_hbm else pltpu.VMEM(o, f32) for o in outs],
        in_specs=[pl.BlockSpec(memory_space=pltpu.VMEM)] * len(args),
        out_specs=[pl.BlockSpec(memory_space=pltpu.VMEM)] * len(outs),
        scratch_shapes=list(scratch),
        compiler_params=pltpu.CompilerParams(vmem_limit_bytes=VMEM_LIMIT),
        cost_estimate=pl.CostEstimate(
            flops=flops, bytes_accessed=4 * sum(math.prod(o) for o in outs), transcendentals=flops // 32
        ),
        name=kernel.__name__,
    )(*[pltpu.with_memory_space_constraint(a, pltpu.VMEM) for a in args])


def shards(states, occupations, core_density):
    f32 = jnp.float32
    parts = lax.axis_size("interval")
    slabs = lax.axis_size("slab")
    planes, rows, cols = core_density.shape
    own = rows // parts
    wide = own + 2 * HALO
    block = (planes, wide, cols)
    pieces = 4
    groups = ((5,), (7,), (3,), (6,), (2,), (4,), (1,), (0,))
    terms = pl.pallas_call(
        functools.partial(terms_kernel, groups),
        out_shape=[pltpu.VMEM((planes * len(group), wide, cols), f32) for group in groups],
        in_specs=[pl.BlockSpec(memory_space=pltpu.HBM)] * 3,
        out_specs=[pl.BlockSpec(memory_space=pltpu.VMEM)] * len(groups),
        scratch_shapes=[
            pltpu.SMEM(occupations.shape, jnp.int32),
            pltpu.VMEM(states.shape, f32),
            pltpu.VMEM((planes, own + 16, cols), f32),
            pltpu.SemaphoreType.DMA((pieces + 4,)),
        ],
        compiler_params=pltpu.CompilerParams(vmem_limit_bytes=VMEM_LIMIT),
        name="terms_kernel",
    )(*[pltpu.with_memory_space_constraint(a, pltpu.HBM) for a in (occupations, states, core_density)])
    swap = lambda a, k: lax.ppermute(a, "interval", [(i, i ^ k) for i in range(parts)])
    got = swap(terms[0], 1)
    other = [swap(terms[1], 6), swap(terms[2], 2)]
    mine = [swap(terms[3], 6), swap(terms[4], 2)]
    crossing = terms[6] + other[0] + other[1]
    across = swap(crossing, 1)
    mine.append(swap(terms[5] + got, 4))
    density = terms[7] + mine[0] + mine[1] + mine[2] + across
    chips = slabs // 2
    beside = lambda q, odd: (q + (1 if q % 2 == odd else -1)) % chips
    odd_pairs = [(s, 2 * beside(s // 2, 1) + 1 - s % 2) for s in range(slabs)]
    even_pairs = [(s, 2 * beside(s // 2, 0) + 1 - s % 2) for s in range(slabs)]
    mates = [(s, s ^ 1) for s in range(slabs)]
    from_even = lax.ppermute(density, "slab", even_pairs)
    from_odd = lax.ppermute(density, "slab", odd_pairs)
    mate = lax.ppermute(density, "slab", mates)
    w, factor, base, change, gx, gy = call(own_kernel, [block] * 6, density, flops=100_000_000)
    from_odd, from_even, w = lax.optimization_barrier((from_odd, from_even, w))
    at = lax.axis_index("slab")
    odd_near = lax.rem(at // 2 + at, 2) == 0
    near = jnp.where(odd_near, from_odd, from_even)
    other = jnp.where(odd_near, from_even, from_odd)[:, :own]
    far = lax.ppermute(other, "slab", mates)
    kept = (planes, own, cols)
    fz, g, twice = call(
        flux_kernel, [kept, block, block], density, mate, near, w, factor, gx, gy, flops=50_000_000
    )
    fz_mate = lax.ppermute(fz, "slab", mates)
    part, w_n, factor_n, flat_n = call(
        flat_kernel, [kept] * 4, density, near, w, factor, base, change, gx, gy, g, twice,
        scratch=[pltpu.VMEM(block, f32)] * 2, flops=100_000_000,
    )
    far, fz_mate, part = lax.optimization_barrier((far, fz_mate, part))
    (out,) = call(
        last_kernel, [kept], density, near, far, part, w_n, factor_n, flat_n, fz, fz_mate, out_hbm=True
    )
    return out


def solution(mesh):
    return jax.shard_map(
        shards,
        mesh=mesh,
        in_specs=(P("interval", "slab", None, None), P("interval"), P("slab", None, None)),
        out_specs=P("slab", "interval", None),
        check_vma=False,
    )
```

```python
import functools
import math

import jax
import jax.numpy as jnp
from jax import lax
from jax.experimental import pallas as pl
from jax.experimental.pallas import tpu as pltpu
from jax.sharding import PartitionSpec as P

spacing = 0.25
denominator = 64.0
kappa = 0.804
mu = 0.2195149727645171
beta = 0.06672455060314922
gamma = (1.0 - math.log(2.0)) / math.pi**2
pw_a = 0.0310907
alpha1 = 0.2137
beta_over_gamma = beta / gamma
exch = 0.75 * (3.0 / math.pi) ** (1.0 / 3.0)
rs_unit = (3.0 / (4.0 * math.pi)) ** (1.0 / 3.0)
s_unit = 1.0 / (4.0 * (3.0 * math.pi**2) ** (2.0 / 3.0))
t_unit = math.pi / (16.0 * (3.0 * math.pi**2) ** (1.0 / 3.0))
q1 = 2.0 * pw_a * 7.5957 * rs_unit**0.5
q2 = 2.0 * pw_a * 3.5876 * rs_unit
q3 = 2.0 * pw_a * 1.6382 * rs_unit**1.5
q4 = 2.0 * pw_a * 0.49294 * rs_unit**2

third = 1.0 / (12.0 * spacing)
HALO = 4
VMEM_LIMIT = 40 * 1024 * 1024


def of_density(n, with_energy):
    w = jnp.exp(jnp.log(n) * (-1.0 / 6.0))
    q = w * (q1 + w * (q2 + w * (q3 + w * q4)))
    radius = rs_unit * (w * w)
    slope = 1.0 + alpha1 * radius
    log_term = jnp.log(1.0 + 1.0 / q)
    e_corr = (-2.0 * pw_a) * slope * log_term
    grown = jnp.exp(e_corr * (-1.0 / gamma))
    less = 1.0 / (grown - 1.0)
    factor = beta_over_gamma * less
    if not with_energy:
        return w, factor
    rq = w * (0.5 * q1 + w * (q2 + w * (1.5 * q3 + w * (2.0 * q4))))
    change = (2.0 * pw_a / 3.0) * (alpha1 * radius * log_term - slope * rq / (q * (q + 1.0)))
    return w, factor, e_corr + change, change * factor * (grown * less) * (1.0 / gamma)


def of_gradient(w, factor, g, energy=None):
    w2 = w * w
    w4 = w2 * w2
    w8 = w4 * w4
    s_sq = (s_unit * g) * (w8 * w8)
    t_sq = (t_unit * g) * (w8 * w4 * w2)
    u = factor * t_sq
    up = 1.0 + u
    d = up + u * u
    wide = d + beta_over_gamma * t_sq * up
    inv = 1.0 / (d * wide)
    h_t = beta * (1.0 + 2.0 * u) * inv
    inv_x = 1.0 / (1.0 + (mu / kappa) * s_sq)
    f_s = mu * inv_x * inv_x
    twice = (2.0 * w8) * (t_unit * h_t - (exch * s_unit) * f_s)
    if energy is None:
        return twice
    n, base, change = energy
    h = gamma * jnp.log(wide * wide * inv)
    h_a = -beta * (t_sq * t_sq) * u * (2.0 + u) * inv
    f_x = (1.0 + kappa) - kappa * inv_x
    e_n = base + h + change * h_a - (7.0 / 3.0) * t_sq * h_t
    e_n = e_n - (4.0 / 3.0 * exch) * (n * w4) * (f_x - 2.0 * s_sq * f_s)
    return twice, e_n


def roll(v, shift, axis):
    return pltpu.roll(v, shift % v.shape[axis], axis)


def d_along(v, axis):
    near = roll(v, -1, axis) - roll(v, 1, axis)
    far = roll(v, -2, axis) - roll(v, 2, axis)
    return (8.0 * third) * near - third * far


def d_z(p2, p1, m1, m2):
    return (8.0 * third) * (p1 - m1) - third * (p2 - m2)


def terms_kernel(groups, occ_ref, states_ref, core_ref, *refs):
    *outs, occ_held, held, core_held, sems = refs
    rows = held.shape[2]
    parts = sum(len(group) for group in groups)
    own = rows // parts
    me = lax.axis_index("interval")
    flip = lax.rem(lax.axis_index("slab"), 2)
    first = pltpu.make_async_copy(occ_ref, occ_held, sems.at[0])
    first.start()
    places = [(k, out, 2 * j) for group, out in zip(groups, outs) for j, k in enumerate(group)]
    copies = []
    for k, _, _ in places:
        at = pl.ds(pl.multiple_of((me ^ k) * own, 8), own)
        copies.append(pltpu.make_async_copy(states_ref.at[:, :, at], held.at[:, :, at], sems.at[4 + k]))
    low = pl.multiple_of(lax.rem(me * own + rows - 8, rows), 8)
    mid = pl.multiple_of(me * own, 8)
    top = pl.multiple_of(lax.rem(me * own + own, rows), 8)
    for k, (start, size, to) in enumerate(((mid, own, 0), (top, 8, own), (low, 8, own + 8))):
        copies.append(
            pltpu.make_async_copy(
                core_ref.at[:, pl.ds(start, size)], core_held.at[:, pl.ds(to, size)], sems.at[1 + k]
            )
        )
    for c in copies:
        c.start()
    first.wait()
    w0 = occ_held[0].astype(jnp.float32) * (1.0 / denominator)
    w1 = occ_held[1].astype(jnp.float32) * (1.0 / denominator)

    def term(p, row):
        at = pl.ds(pl.multiple_of(row, 8), 8)
        a, b = held[0, p, at], held[1, p, at]
        return w0 * a * a + w1 * b * b

    for (k, out, shift), copy in zip(places, copies):
        copy.wait()
        if k == 0:
            for c in copies[parts:]:
                c.wait()
        for p in range(2):
            for r in range(0, own, 8):
                t = term(p, (me ^ k) * own + r)
                if k == 0:
                    t = t + core_held[p, pl.ds(r, 8)]
                out[shift + (p ^ flip), pl.ds(r, 8)] = t
    for k, out, shift in places:
        i = me ^ k
        up = lax.rem(i + 1, parts) * own
        down = lax.rem(i + parts - 1, parts) * own + own - 8
        for p in range(2):
            to = shift + (p ^ flip)
            t, b = term(p, up), term(p, down)
            if k == 0:
                t, b = t + core_held[p, pl.ds(own, 8)], b + core_held[p, pl.ds(own + 8, 8)]
            out[to, pl.ds(own, HALO)] = t[:HALO]
            out[to, pl.ds(own + HALO, HALO)] = b[HALO:]


def x_slopes(field, slopes):
    for p in range(2):
        for c in range(0, field.shape[2], 128):
            at = pl.ds(c, 128)
            slopes[p, :, at] = d_along(field[p, :, at], 0)


def own_kernel(s_ref, w_ref, a_ref, base_ref, change_ref, gx_ref, gy_ref):
    x_slopes(s_ref, gx_ref)
    for p in range(2):
        for r in range(0, s_ref.shape[1], 8):
            at = pl.ds(r, 8)
            n = s_ref[p, at]
            gy_ref[p, at] = d_along(n, 1)
            if r < s_ref.shape[1] - 2 * HALO:
                w_ref[p, at], a_ref[p, at], base_ref[p, at], change_ref[p, at] = of_density(n, True)
            else:
                w_ref[p, at], a_ref[p, at] = of_density(n, False)


def flux_kernel(s_ref, m_ref, n_ref, w_ref, a_ref, gx_ref, gy_ref, fz_ref, g_ref, twice_ref):
    rows = s_ref.shape[1]
    own = rows - 2 * HALO
    for r in range(0, rows, 8):
        at = pl.ds(r, 8)
        s = (s_ref[0, at], s_ref[1, at], m_ref[1, at], m_ref[0, at])
        n = (n_ref[0, at], n_ref[1, at])
        for p, gz in ((0, d_z(s[2], s[1], n[0], n[1])), (1, d_z(s[3], s[2], s[0], n[0]))):
            gx, gy = gx_ref[p, at], gy_ref[p, at]
            g = gz * gz + gx * gx + gy * gy
            twice = of_gradient(w_ref[p, at], a_ref[p, at], g)
            g_ref[p, at] = g
            twice_ref[p, at] = twice
            if r < own:
                fz_ref[p, at] = twice * gz


def flat_kernel(
    s_ref, n_ref, w_ref, a_ref, base_ref, change_ref, gx_ref, gy_ref, g_ref, twice_ref,
    part_ref, wn_ref, an_ref, flat_ref, slopes, fx
):
    rows = s_ref.shape[1]
    own = rows - 2 * HALO
    for p in range(2):
        for r in range(0, rows, 8):
            at = pl.ds(r, 8)
            fx[p, at] = twice_ref[p, at] * gx_ref[p, at]
    x_slopes(fx, slopes)
    x_slopes(n_ref, fx)
    for r in range(0, own, 8):
        at = pl.ds(r, 8)
        for p in range(2):
            _, e_n = of_gradient(
                w_ref[p, at], a_ref[p, at], g_ref[p, at], (s_ref[p, at], base_ref[p, at], change_ref[p, at])
            )
            part_ref[p, at] = e_n - slopes[p, at] - d_along(twice_ref[p, at] * gy_ref[p, at], 1)
            n = n_ref[p, at]
            gx, gy = fx[p, at], d_along(n, 1)
            flat_ref[p, at] = gx * gx + gy * gy
            wn_ref[p, at], an_ref[p, at] = of_density(n, False)


def last_kernel(s_ref, n_ref, b_ref, part_ref, wn_ref, an_ref, flat_ref, fz_ref, fm_ref, out_ref, held, sems):
    own = part_ref.shape[1]
    flip = lax.rem(lax.axis_index("slab"), 2)
    copies = []
    for r in range(0, own, 8):
        at = pl.ds(r, 8)
        s = (s_ref[0, at], s_ref[1, at])
        n = (n_ref[0, at], n_ref[1, at], b_ref[1, at], b_ref[0, at])
        f = []
        for p, gz in ((0, d_z(s[1], s[0], n[1], n[2])), (1, d_z(s[0], n[0], n[2], n[3]))):
            f.append(of_gradient(wn_ref[p, at], an_ref[p, at], gz * gz + flat_ref[p, at]) * gz)
        f0, f1 = fz_ref[0, at], fz_ref[1, at]
        f2, f3 = -fm_ref[1, at], -fm_ref[0, at]
        held[flip, at] = part_ref[0, at] - d_z(f2, f1, f[0], f[1])
        held[1 - flip, at] = part_ref[1, at] - d_z(f3, f2, f0, f[0])
        copies.append(pltpu.make_async_copy(held.at[:, at], out_ref.at[:, at], sems.at[r // 8]))
        copies[-1].start()
    for c in copies:
        c.wait()


def call(kernel, outs, *args, scratch=(), out_hbm=False, flops=0):
    f32 = jnp.float32
    return pl.pallas_call(
        kernel,
        out_shape=[jax.ShapeDtypeStruct(o, f32) if out_hbm else pltpu.VMEM(o, f32) for o in outs],
        in_specs=[pl.BlockSpec(memory_space=pltpu.VMEM)] * len(args),
        out_specs=[pl.BlockSpec(memory_space=pl.ANY if out_hbm else pltpu.VMEM)] * len(outs),
        scratch_shapes=list(scratch),
        compiler_params=pltpu.CompilerParams(vmem_limit_bytes=VMEM_LIMIT),
        cost_estimate=pl.CostEstimate(
            flops=flops, bytes_accessed=4 * sum(math.prod(o) for o in outs), transcendentals=flops // 32
        ),
        name=kernel.__name__,
    )(*[pltpu.with_memory_space_constraint(a, pltpu.VMEM) for a in args])


def shards(states, occupations, core_density):
    f32 = jnp.float32
    parts = lax.axis_size("interval")
    slabs = lax.axis_size("slab")
    planes, rows, cols = core_density.shape
    own = rows // parts
    wide = own + 2 * HALO
    block = (planes, wide, cols)
    groups = ((5,), (7,), (3,), (6,), (2,), (4,), (1,), (0,))
    terms = pl.pallas_call(
        functools.partial(terms_kernel, groups),
        out_shape=[pltpu.VMEM((planes * len(group), wide, cols), f32) for group in groups],
        in_specs=[pl.BlockSpec(memory_space=pltpu.HBM)] * 3,
        out_specs=[pl.BlockSpec(memory_space=pltpu.VMEM)] * len(groups),
        scratch_shapes=[
            pltpu.SMEM(occupations.shape, jnp.int32),
            pltpu.VMEM(states.shape, f32),
            pltpu.VMEM((planes, own + 16, cols), f32),
            pltpu.SemaphoreType.DMA((parts + 4,)),
        ],
        compiler_params=pltpu.CompilerParams(vmem_limit_bytes=VMEM_LIMIT),
        name="terms_kernel",
    )(*[pltpu.with_memory_space_constraint(a, pltpu.HBM) for a in (occupations, states, core_density)])
    swap = lambda a, k: lax.ppermute(a, "interval", [(i, i ^ k) for i in range(parts)])
    got = swap(terms[0], 1)
    other = [swap(terms[1], 6), swap(terms[2], 2)]
    mine = [swap(terms[3], 6), swap(terms[4], 2)]
    crossing = terms[6] + other[0] + other[1]
    across = swap(crossing, 1)
    mine.append(swap(terms[5] + got, 4))
    density = terms[7] + mine[0] + mine[1] + mine[2] + across
    chips = slabs // 2
    beside = lambda q, odd: (q + (1 if q % 2 == odd else -1)) % chips
    odd_pairs = [(s, 2 * beside(s // 2, 1) + 1 - s % 2) for s in range(slabs)]
    even_pairs = [(s, 2 * beside(s // 2, 0) + 1 - s % 2) for s in range(slabs)]
    mates = [(s, s ^ 1) for s in range(slabs)]
    low_end = lambda q: q % (chips // 2) < 2
    first = [pair if low_end(pair[0] // 2) else (pair[0], pair[0]) for pair in even_pairs]
    last = [(pair[0], pair[0]) if low_end(pair[0] // 2) else pair for pair in even_pairs]
    from_first = lax.ppermute(density, "slab", first)
    from_odd = lax.ppermute(density, "slab", odd_pairs)
    from_last = lax.ppermute(density, "slab", last)
    mate = lax.ppermute(density, "slab", mates)
    w, factor, base, change, gx, gy = call(own_kernel, [block] * 6, density, flops=100_000_000)
    from_last, from_odd, from_first, w = lax.optimization_barrier((from_last, from_odd, from_first, w))
    at = lax.axis_index("slab")
    at_end = low_end(at // 2)
    from_even = jnp.where(at_end, from_first, from_last)
    odd_near = lax.rem(at // 2 + at, 2) == 0
    near = jnp.where(odd_near, from_odd, from_even)
    other = jnp.where(odd_near, from_even, from_odd)[:, :own]
    kept = (planes, own, cols)
    fz, g, twice = call(
        flux_kernel, [kept, block, block], density, mate, near, w, factor, gx, gy, flops=50_000_000
    )
    to_mate, other = lax.optimization_barrier((fz, other))
    far = lax.ppermute(other, "slab", mates)
    fz_mate = lax.ppermute(to_mate, "slab", mates)
    part, w_n, factor_n, flat_n = call(
        flat_kernel, [kept] * 4, density, near, w, factor, base, change, gx, gy, g, twice,
        scratch=[pltpu.VMEM(block, f32)] * 2, flops=100_000_000,
    )
    far, fz_mate, part = lax.optimization_barrier((far, fz_mate, part))
    (out,) = call(
        last_kernel, [kept], density, near, far, part, w_n, factor_n, flat_n, fz, fz_mate, out_hbm=True,
        scratch=[pltpu.VMEM(kept, f32), pltpu.SemaphoreType.DMA((own // 8,))],
    )
    return out


def solution(mesh):
    return jax.shard_map(
        shards,
        mesh=mesh,
        in_specs=(P("interval", "slab", None, None), P("interval"), P("slab", None, None)),
        out_specs=P("slab", "interval", None),
        check_vma=False,
    )
```

```python
import functools
import math

import jax
import jax.numpy as jnp
from jax import lax
from jax.experimental import pallas as pl
from jax.experimental.pallas import tpu as pltpu
from jax.sharding import PartitionSpec as P

spacing = 0.25
denominator = 64.0
kappa = 0.804
mu = 0.2195149727645171
beta = 0.06672455060314922
gamma = (1.0 - math.log(2.0)) / math.pi**2
pw_a = 0.0310907
alpha1 = 0.2137
beta_over_gamma = beta / gamma
exch = 0.75 * (3.0 / math.pi) ** (1.0 / 3.0)
rs_unit = (3.0 / (4.0 * math.pi)) ** (1.0 / 3.0)
s_unit = 1.0 / (4.0 * (3.0 * math.pi**2) ** (2.0 / 3.0))
t_unit = math.pi / (16.0 * (3.0 * math.pi**2) ** (1.0 / 3.0))
q1 = 2.0 * pw_a * 7.5957 * rs_unit**0.5
q2 = 2.0 * pw_a * 3.5876 * rs_unit
q3 = 2.0 * pw_a * 1.6382 * rs_unit**1.5
q4 = 2.0 * pw_a * 0.49294 * rs_unit**2

third = 1.0 / (12.0 * spacing)
HALO = 4
VMEM_LIMIT = 40 * 1024 * 1024


def of_density(n, with_energy):
    w = jnp.exp(jnp.log(n) * (-1.0 / 6.0))
    q = w * (q1 + w * (q2 + w * (q3 + w * q4)))
    radius = rs_unit * (w * w)
    slope = 1.0 + alpha1 * radius
    log_term = jnp.log(1.0 + 1.0 / q)
    e_corr = (-2.0 * pw_a) * slope * log_term
    grown = jnp.exp(e_corr * (-1.0 / gamma))
    less = 1.0 / (grown - 1.0)
    factor = beta_over_gamma * less
    if not with_energy:
        return w, factor
    rq = w * (0.5 * q1 + w * (q2 + w * (1.5 * q3 + w * (2.0 * q4))))
    change = (2.0 * pw_a / 3.0) * (alpha1 * radius * log_term - slope * rq / (q * (q + 1.0)))
    return w, factor, e_corr + change, change * factor * (grown * less) * (1.0 / gamma)


def of_gradient(w, factor, g, energy=None):
    w2 = w * w
    w4 = w2 * w2
    w8 = w4 * w4
    s_sq = (s_unit * g) * (w8 * w8)
    t_sq = (t_unit * g) * (w8 * w4 * w2)
    u = factor * t_sq
    up = 1.0 + u
    d = up + u * u
    wide = d + beta_over_gamma * t_sq * up
    inv = 1.0 / (d * wide)
    h_t = beta * (1.0 + 2.0 * u) * inv
    inv_x = 1.0 / (1.0 + (mu / kappa) * s_sq)
    f_s = mu * inv_x * inv_x
    twice = (2.0 * w8) * (t_unit * h_t - (exch * s_unit) * f_s)
    if energy is None:
        return twice
    n, base, change = energy
    h = gamma * jnp.log(wide * wide * inv)
    h_a = -beta * (t_sq * t_sq) * u * (2.0 + u) * inv
    f_x = (1.0 + kappa) - kappa * inv_x
    e_n = base + h + change * h_a - (7.0 / 3.0) * t_sq * h_t
    e_n = e_n - (4.0 / 3.0 * exch) * (n * w4) * (f_x - 2.0 * s_sq * f_s)
    return twice, e_n


def roll(v, shift, axis):
    return pltpu.roll(v, shift % v.shape[axis], axis)


def d_along(v, axis):
    near = roll(v, -1, axis) - roll(v, 1, axis)
    far = roll(v, -2, axis) - roll(v, 2, axis)
    return (8.0 * third) * near - third * far


def d_z(p2, p1, m1, m2):
    return (8.0 * third) * (p1 - m1) - third * (p2 - m2)


def terms_kernel(groups, occ_ref, states_ref, core_ref, *refs):
    *outs, occ_held, held, core_held, sems = refs
    rows = held.shape[2]
    parts = sum(len(group) for group in groups)
    own = rows // parts
    me = lax.axis_index("interval")
    flip = lax.rem(lax.axis_index("slab"), 2)
    first = pltpu.make_async_copy(occ_ref, occ_held, sems.at[0])
    first.start()
    places = [(k, out, 2 * j) for group, out in zip(groups, outs) for j, k in enumerate(group)]
    copies = []
    for k, _, _ in places:
        at = pl.ds(pl.multiple_of((me ^ k) * own, 8), own)
        copies.append(pltpu.make_async_copy(states_ref.at[:, :, at], held.at[:, :, at], sems.at[4 + k]))
    low = pl.multiple_of(lax.rem(me * own + rows - 8, rows), 8)
    mid = pl.multiple_of(me * own, 8)
    top = pl.multiple_of(lax.rem(me * own + own, rows), 8)
    for k, (start, size, to) in enumerate(((mid, own, 0), (top, 8, own), (low, 8, own + 8))):
        copies.append(
            pltpu.make_async_copy(
                core_ref.at[:, pl.ds(start, size)], core_held.at[:, pl.ds(to, size)], sems.at[1 + k]
            )
        )
    for c in copies:
        c.start()
    first.wait()
    w0 = occ_held[0].astype(jnp.float32) * (1.0 / denominator)
    w1 = occ_held[1].astype(jnp.float32) * (1.0 / denominator)

    def term(p, row):
        at = pl.ds(pl.multiple_of(row, 8), 8)
        a, b = held[0, p, at], held[1, p, at]
        return w0 * a * a + w1 * b * b

    for (k, out, shift), copy in zip(places, copies):
        copy.wait()
        if k == 0:
            for c in copies[parts:]:
                c.wait()
        for p in range(2):
            for r in range(0, own, 8):
                t = term(p, (me ^ k) * own + r)
                if k == 0:
                    t = t + core_held[p, pl.ds(r, 8)]
                out[shift + (p ^ flip), pl.ds(r, 8)] = t
    for k, out, shift in places:
        i = me ^ k
        up = lax.rem(i + 1, parts) * own
        down = lax.rem(i + parts - 1, parts) * own + own - 8
        for p in range(2):
            to = shift + (p ^ flip)
            t, b = term(p, up), term(p, down)
            if k == 0:
                t, b = t + core_held[p, pl.ds(own, 8)], b + core_held[p, pl.ds(own + 8, 8)]
            out[to, pl.ds(own, HALO)] = t[:HALO]
            out[to, pl.ds(own + HALO, HALO)] = b[HALO:]


def x_slopes(field, slopes):
    for p in range(2):
        for c in range(0, field.shape[2], 128):
            at = pl.ds(c, 128)
            slopes[p, :, at] = d_along(field[p, :, at], 0)


def own_kernel(s_ref, w_ref, a_ref, base_ref, change_ref, gx_ref, gy_ref):
    x_slopes(s_ref, gx_ref)
    for p in range(2):
        for r in range(0, s_ref.shape[1], 8):
            at = pl.ds(r, 8)
            n = s_ref[p, at]
            gy_ref[p, at] = d_along(n, 1)
            if r < s_ref.shape[1] - 2 * HALO:
                w_ref[p, at], a_ref[p, at], base_ref[p, at], change_ref[p, at] = of_density(n, True)
            else:
                w_ref[p, at], a_ref[p, at] = of_density(n, False)


def flux_kernel(s_ref, m_ref, n_ref, w_ref, a_ref, gx_ref, gy_ref, fz_ref, g_ref, twice_ref):
    rows = s_ref.shape[1]
    own = rows - 2 * HALO
    for r in range(0, rows, 8):
        at = pl.ds(r, 8)
        s = (s_ref[0, at], s_ref[1, at], m_ref[1, at], m_ref[0, at])
        n = (n_ref[0, at], n_ref[1, at])
        for p, gz in ((0, d_z(s[2], s[1], n[0], n[1])), (1, d_z(s[3], s[2], s[0], n[0]))):
            gx, gy = gx_ref[p, at], gy_ref[p, at]
            g = gz * gz + gx * gx + gy * gy
            twice = of_gradient(w_ref[p, at], a_ref[p, at], g)
            g_ref[p, at] = g
            twice_ref[p, at] = twice
            if r < own:
                fz_ref[p, at] = twice * gz


def flat_kernel(
    s_ref, n_ref, w_ref, a_ref, base_ref, change_ref, gx_ref, gy_ref, g_ref, twice_ref,
    part_ref, wn_ref, an_ref, flat_ref, slopes, fx
):
    rows = s_ref.shape[1]
    own = rows - 2 * HALO
    for p in range(2):
        for r in range(0, rows, 8):
            at = pl.ds(r, 8)
            fx[p, at] = twice_ref[p, at] * gx_ref[p, at]
    x_slopes(fx, slopes)
    x_slopes(n_ref, fx)
    for r in range(0, own, 8):
        at = pl.ds(r, 8)
        for p in range(2):
            _, e_n = of_gradient(
                w_ref[p, at], a_ref[p, at], g_ref[p, at], (s_ref[p, at], base_ref[p, at], change_ref[p, at])
            )
            part_ref[p, at] = e_n - slopes[p, at] - d_along(twice_ref[p, at] * gy_ref[p, at], 1)
            n = n_ref[p, at]
            gx, gy = fx[p, at], d_along(n, 1)
            flat_ref[p, at] = gx * gx + gy * gy
            wn_ref[p, at], an_ref[p, at] = of_density(n, False)


def last_kernel(s_ref, n_ref, b_ref, part_ref, wn_ref, an_ref, flat_ref, fz_ref, fm_ref, out_ref, held, sems):
    own = part_ref.shape[1]
    flip = lax.rem(lax.axis_index("slab"), 2)
    copies = []
    for r in range(0, own, 8):
        at = pl.ds(r, 8)
        s = (s_ref[0, at], s_ref[1, at])
        n = (n_ref[0, at], n_ref[1, at], b_ref[1, at], b_ref[0, at])
        f = []
        for p, gz in ((0, d_z(s[1], s[0], n[1], n[2])), (1, d_z(s[0], n[0], n[2], n[3]))):
            f.append(of_gradient(wn_ref[p, at], an_ref[p, at], gz * gz + flat_ref[p, at]) * gz)
        f0, f1 = fz_ref[0, at], fz_ref[1, at]
        f2, f3 = -fm_ref[1, at], -fm_ref[0, at]
        held[flip, at] = part_ref[0, at] - d_z(f2, f1, f[0], f[1])
        held[1 - flip, at] = part_ref[1, at] - d_z(f3, f2, f0, f[0])
        copies.append(pltpu.make_async_copy(held.at[:, at], out_ref.at[:, at], sems.at[r // 8]))
        copies[-1].start()
    for c in copies:
        c.wait()


def call(kernel, outs, *args, scratch=(), out_hbm=False, flops=0):
    f32 = jnp.float32
    return pl.pallas_call(
        kernel,
        out_shape=[jax.ShapeDtypeStruct(o, f32) if out_hbm else pltpu.VMEM(o, f32) for o in outs],
        in_specs=[pl.BlockSpec(memory_space=pltpu.VMEM)] * len(args),
        out_specs=[pl.BlockSpec(memory_space=pl.ANY if out_hbm else pltpu.VMEM)] * len(outs),
        scratch_shapes=list(scratch),
        compiler_params=pltpu.CompilerParams(vmem_limit_bytes=VMEM_LIMIT),
        cost_estimate=pl.CostEstimate(
            flops=flops, bytes_accessed=4 * sum(math.prod(o) for o in outs), transcendentals=flops // 32
        ),
        name=kernel.__name__,
    )(*[pltpu.with_memory_space_constraint(a, pltpu.VMEM) for a in args])


def shards(states, occupations, core_density):
    f32 = jnp.float32
    parts = lax.axis_size("interval")
    slabs = lax.axis_size("slab")
    planes, rows, cols = core_density.shape
    own = rows // parts
    wide = own + 2 * HALO
    block = (planes, wide, cols)
    groups = ((5,), (7,), (3,), (6,), (2,), (4,), (1,), (0,))
    terms = pl.pallas_call(
        functools.partial(terms_kernel, groups),
        out_shape=[pltpu.VMEM((planes * len(group), wide, cols), f32) for group in groups],
        in_specs=[pl.BlockSpec(memory_space=pltpu.HBM)] * 3,
        out_specs=[pl.BlockSpec(memory_space=pltpu.VMEM)] * len(groups),
        scratch_shapes=[
            pltpu.SMEM(occupations.shape, jnp.int32),
            pltpu.VMEM(states.shape, f32),
            pltpu.VMEM((planes, own + 16, cols), f32),
            pltpu.SemaphoreType.DMA((parts + 4,)),
        ],
        compiler_params=pltpu.CompilerParams(vmem_limit_bytes=VMEM_LIMIT),
        name="terms_kernel",
    )(*[pltpu.with_memory_space_constraint(a, pltpu.HBM) for a in (occupations, states, core_density)])
    swap = lambda a, k: lax.ppermute(a, "interval", [(i, i ^ k) for i in range(parts)])
    other = [swap(terms[1], 6), swap(terms[2], 2)]
    got, to_2 = lax.optimization_barrier((swap(terms[0], 1), terms[4]))
    far = swap(terms[5] + got, 4)
    mine = [swap(terms[3], 6), swap(to_2, 2)]
    crossing = terms[6] + other[0] + other[1]
    across = swap(crossing, 1)
    density = terms[7] + sum(mine[1:], mine[0]) + far + across
    chips = slabs // 2
    beside = lambda q, odd: (q + (1 if q % 2 == odd else -1)) % chips
    odd_pairs = [(s, 2 * beside(s // 2, 1) + 1 - s % 2) for s in range(slabs)]
    even_pairs = [(s, 2 * beside(s // 2, 0) + 1 - s % 2) for s in range(slabs)]
    mates = [(s, s ^ 1) for s in range(slabs)]
    low_end = lambda q: q % (chips // 2) < 2
    first = [pair if low_end(pair[0] // 2) else (pair[0], pair[0]) for pair in even_pairs]
    last = [(pair[0], pair[0]) if low_end(pair[0] // 2) else pair for pair in even_pairs]
    from_first = lax.ppermute(density, "slab", first)
    from_odd = lax.ppermute(density, "slab", odd_pairs)
    from_last = lax.ppermute(density, "slab", last)
    mate = lax.ppermute(density, "slab", mates)
    w, factor, base, change, gx, gy = call(own_kernel, [block] * 6, density, flops=100_000_000)
    from_last, from_odd, from_first, w = lax.optimization_barrier((from_last, from_odd, from_first, w))
    at = lax.axis_index("slab")
    at_end = low_end(at // 2)
    from_even = jnp.where(at_end, from_first, from_last)
    odd_near = lax.rem(at // 2 + at, 2) == 0
    near = jnp.where(odd_near, from_odd, from_even)
    other = jnp.where(odd_near, from_even, from_odd)[:, :own]
    kept = (planes, own, cols)
    fz, g, twice = call(
        flux_kernel, [kept, block, block], density, mate, near, w, factor, gx, gy, flops=50_000_000
    )
    to_mate, other = lax.optimization_barrier((fz, other))
    far = lax.ppermute(other, "slab", mates)
    fz_mate = lax.ppermute(to_mate, "slab", mates)
    part, w_n, factor_n, flat_n = call(
        flat_kernel, [kept] * 4, density, near, w, factor, base, change, gx, gy, g, twice,
        scratch=[pltpu.VMEM(block, f32)] * 2, flops=100_000_000,
    )
    far, fz_mate, part = lax.optimization_barrier((far, fz_mate, part))
    (out,) = call(
        last_kernel, [kept], density, near, far, part, w_n, factor_n, flat_n, fz, fz_mate, out_hbm=True,
        scratch=[pltpu.VMEM(kept, f32), pltpu.SemaphoreType.DMA((own // 8,))],
    )
    return out


def solution(mesh):
    return jax.shard_map(
        shards,
        mesh=mesh,
        in_specs=(P("interval", "slab", None, None), P("interval"), P("slab", None, None)),
        out_specs=P("slab", "interval", None),
        check_vma=False,
    )
```
